512 devices in a mesh: dp: 32 (over y, z_hi), mp: 16 (over z_lo, x, core).
Axes of the slice: x: 4, y: 8, z: 8 (z_hi: 4, z_lo: 2; z = z_hi * 2 + z_lo), core: 2. Of those that a mesh axis runs over, the one named last changes fastest.
Arguments:
- image_emb: bfloat16 [16384, 1152], P('dp'), may hold values from -6 to 6
- text_emb: bfloat16 [16384, 1152], P(('dp', 'mp')), may hold values from -6 to 6
- image_feat: bfloat16 [16384, 1152], P('dp'), may hold values from -6 to 6
- text_feat: bfloat16 [16384, 1152], P('dp'), may hold values from -6 to 6
- logit_scale: float32 [1], replicated, may hold values from 4 to 16
- logit_bias: float32 [1], replicated, may hold values from -8 to -2
Outputs:
- image_proj_grad: float32 [1152, 1152], P('dp', 'mp')
- text_proj_grad: float32 [1152, 1152], P('dp', 'mp')
The draws below stay inside these ranges and needn't reach their ends.
All inputs are finite; a program needn't handle non-finite values.
Results may differ from the reference program's by a relative error of at most 0.0055.
Values may be sent and summed in bfloat16 or wider, within the bound.
No kernel may reach another device: no remote copies, remote signals or barrier semaphores. Data moves between devices by JAX's collectives and lax.ppermute only.
A program may use at most 64 MiB of HBM per device.

```python
import math
import jax
import jax.numpy as jnp
from jax import lax

D = 1152
E = 1152
ROWS_DEV = 32
BATCH = 16384
N_DP = 32
N_MP = 16


def spiked(values, rng, source, target, blocks, factor):
    owner, partner = [(jnp.arange(values.shape[axis_at]) // (values.shape[axis_at] // blocks)).reshape([-1 if axis == axis_at else 1 for axis in range(values.ndim)]) for axis_at in (source, target)]
    chosen = jax.random.permutation(rng, blocks)[partner]
    strong = (owner == chosen) | (owner == (partner + blocks // 2) % blocks)
    return jnp.where(strong, factor * values, values)


def shard_levels(key, dims, shards, least, largest):
    level = 1.0
    for axis_at, blocks in shards:
        heights = jax.random.uniform(jax.random.fold_in(jax.random.fold_in(key, 6), axis_at), (blocks,), jnp.float32, least / len(shards), largest / len(shards))
        level = level * jnp.repeat(jnp.exp(heights), dims[axis_at] // blocks).reshape((-1,) + (1,) * (len(dims) - 1 - axis_at))
    return level


def noise(rng, dims, scale, most, pieces=(), held_as=jnp.bfloat16):
    loudness = shard_levels(rng, dims, pieces, -0.22, 0.18) if pieces else 1.0
    entries = jax.random.normal(rng, dims, jnp.float32) * scale * loudness
    return jnp.minimum(jnp.maximum(entries, -most), most).astype(held_as)


def gaussian_with(stream_key, shape, deviation, bound, shards, heavy, kind=jnp.bfloat16):
    entries = deviation * jax.random.normal(stream_key, shape, jnp.float32)
    if shards:
        entries = entries * shard_levels(stream_key, shape, shards, -0.22, 0.18)
    return jnp.clip(spiked(entries, jax.random.fold_in(stream_key, 3), *heavy), -bound, bound).astype(kind)


def setup_inputs(seed: int = 0) -> dict:
    splits = jax.random.split(jax.random.key(seed), 7)
    image_emb = noise(splits[0], (BATCH, E), 1.0, 6.0, ((0, 32),))
    text_emb = noise(splits[1], (BATCH, E), 1.0, 6.0, ((0, 512),))
    image_feat = gaussian_with(splits[2], (BATCH, D), 1.0, 6.0, ((0, 32),), (0, 1, 32, 2.75))
    text_feat = gaussian_with(splits[3], (BATCH, D), 1.0, 6.0, ((0, 32),), (0, 1, 32, 2.75))
    logit_scale = jnp.clip(jnp.exp(jax.random.uniform(splits[4], (1,), jnp.float32, math.log(4.0), math.log(16.0))), 4.0, 16.0)
    logit_bias = jnp.clip(jax.random.uniform(splits[5], (1,), jnp.float32, -8.0, -2.0), -8.0, -2.0)
    return {"image_emb": image_emb, "text_emb": text_emb, "image_feat": image_feat, "text_feat": text_feat, "logit_scale": logit_scale, "logit_bias": logit_bias}


def normalize(rows):
    wide = rows.astype(jnp.float32)
    factor = lax.rsqrt(lax.optimization_barrier(jnp.sum(wide * wide, axis=-1, keepdims=True)) + 1e-06)
    return (wide * factor, factor)

def unit_back(direction, unit, factor):
    return (direction - unit * lax.optimization_barrier(jnp.sum(unit * direction, axis=-1, keepdims=True))) * factor

def reference(image_emb, text_emb, image_feat, text_feat, logit_scale, logit_bias):
    image_unit, image_norm = normalize(image_emb)
    text_unit, text_norm = normalize(text_emb)
    image_low = image_unit.astype(jnp.bfloat16)
    text_low = text_unit.astype(jnp.bfloat16)
    batch = image_low.shape[0]
    width = image_low.shape[1]
    block = ROWS_DEV * N_MP
    scale = logit_scale[0]
    offset = logit_bias[0]
    image_ids = jnp.arange(batch, dtype=jnp.int32)[None, :]

    def one_block(image_dir, start):
        rows = lax.dynamic_slice_in_dim(text_low, start, block, 0)
        logits = lax.dot_general(rows, image_low, (((1,), (1,)), ((), ())), preferred_element_type=jnp.float32)
        text_ids = start + jnp.arange(block, dtype=jnp.int32)[:, None]
        sign = jnp.where(text_ids == image_ids, 1.0, -1.0).astype(jnp.float32)
        value = scale * logits + offset
        weights = (-scale * sign * jax.nn.sigmoid(-sign * value)).astype(jnp.bfloat16)
        text_dir = jnp.dot(weights, image_low, preferred_element_type=jnp.float32)
        image_dir = image_dir + jnp.dot(weights.T, rows, preferred_element_type=jnp.float32)
        return (image_dir, text_dir)
    starts = jnp.arange(N_DP, dtype=jnp.int32) * block
    image_dir, text_dirs = lax.scan(one_block, jnp.zeros((batch, width), jnp.float32), starts)
    text_dir = text_dirs.reshape(batch, width)
    image_grad = unit_back(image_dir, image_unit, image_norm).astype(jnp.bfloat16)
    text_grad = unit_back(text_dir, text_unit, text_norm).astype(jnp.bfloat16)
    image_proj_grad = jnp.dot(image_feat.T, image_grad, preferred_element_type=jnp.float32)
    text_proj_grad = jnp.dot(text_feat.T, text_grad, preferred_element_type=jnp.float32)
    return (image_proj_grad, text_proj_grad)
```

```python
import jax
import jax.numpy as jnp
from jax import lax
from jax.sharding import Mesh, PartitionSpec as P

SIZES = (8, 4, 2, 4, 2)
NAMES = ("y", "zh", "zl", "x", "c")
DP = ("y", "zh")
MP = ("zl", "x", "c")


def shifted(value, axis, steps):
    count = lax.axis_size(axis)
    return lax.ppermute(value, axis, [(s, (s + steps) % count) for s in range(count)])


def normalize(rows):
    wide = rows.astype(jnp.float32)
    factor = lax.rsqrt(jnp.sum(wide * wide, axis=-1, keepdims=True) + 1e-06)
    return (wide * factor, factor)


def unit_back(direction, unit, factor):
    return (direction - unit * jnp.sum(unit * direction, axis=-1, keepdims=True)) * factor


def gather(own, up_last):
    near = [own] + [shifted(own, "zh", k) for k in (1, 2, 3)]
    chunk = jnp.concatenate(near, axis=0)
    chunks = [chunk]
    up = down = chunk
    for _ in range(3):
        up, down = shifted(up, "y", 1), shifted(down, "y", -1)
        chunks += [up, down]
    chunks.append(shifted(up, "y", 1) if up_last else shifted(down, "y", -1))
    return jnp.concatenate(chunks, axis=0)


def sum_over_mp(parts):
    slabs = parts.reshape((8, 2) + parts.shape[1:])
    core = lax.axis_index("c")
    keep = lax.dynamic_index_in_dim(slabs, core, 1, keepdims=False)
    give = lax.dynamic_index_in_dim(slabs, 1 - core, 1, keepdims=False).astype(jnp.bfloat16)
    half = keep + shifted(give, "c", 1).astype(jnp.float32)
    got = lax.all_to_all(half.astype(jnp.bfloat16), ("zl", "x"), 0, 0, tiled=True)
    return jnp.sum(got.astype(jnp.float32), axis=0)


def sum_over_dp(parts):
    slabs = parts.reshape((8, 4) + parts.shape[1:]).astype(jnp.bfloat16)
    got = lax.all_to_all(slabs, "y", 0, 0, tiled=True)
    near = jnp.sum(got.astype(jnp.float32), axis=0)
    return jnp.sum(lax.all_to_all(near, "zh", 0, 0, tiled=True), axis=0)


def local(image_emb, text_emb, image_feat, text_feat, logit_scale, logit_bias):
    column = lax.axis_index(MP)
    own_rows, width = text_emb.shape
    block = image_emb.shape[0]
    depth = image_feat.shape[1]
    scale = logit_scale[0]
    offset = logit_bias[0]
    own_feat = lax.dynamic_slice_in_dim(text_feat, column * own_rows, own_rows, 0)
    all_emb = gather(text_emb, True)
    all_feat = gather(own_feat, False)

    image_unit, image_norm = normalize(image_emb)
    text_unit, text_norm = normalize(all_emb)
    image_low = image_unit.astype(jnp.bfloat16)
    text_low = text_unit.astype(jnp.bfloat16)
    rows = text_low.shape[0]
    logits = lax.dot_general(text_low, image_low, (((1,), (1,)), ((), ())), preferred_element_type=jnp.float32)
    row_ids = jnp.arange(rows, dtype=jnp.int32)[:, None]
    match = (row_ids < own_rows) & (column * own_rows + row_ids == jnp.arange(block, dtype=jnp.int32)[None, :])
    sign = jnp.where(match, 1.0, -1.0).astype(jnp.float32)
    value = scale * logits + offset
    weights = (-scale * sign * jax.nn.sigmoid(-sign * value)).astype(jnp.bfloat16)

    image_dir = lax.dot_general(weights, text_low, (((0,), (0,)), ((), ())), preferred_element_type=jnp.float32)
    image_part = unit_back(image_dir, image_unit, image_norm)
    image_cols = sum_over_mp(image_part.T.reshape(16, width // 16, block)).astype(jnp.bfloat16)
    image_term = jnp.dot(image_cols, image_feat, preferred_element_type=jnp.float32)

    text_dir = jnp.dot(weights, image_low, preferred_element_type=jnp.float32)
    text_part = unit_back(text_dir, text_unit, text_norm).astype(jnp.bfloat16)
    text_all = lax.dot_general(text_part, all_feat, (((0,), (0,)), ((), ())), preferred_element_type=jnp.float32)
    text_term = sum_over_mp(text_all.reshape(16, width // 16, depth))

    def home(term):
        own = sum_over_dp(term.T.reshape(32, depth // 32, width // 16))
        return own

    return (home(image_term), home(text_term))


def solution(mesh):
    split = Mesh(mesh.devices.reshape(SIZES), NAMES)
    in_specs = (P(DP, None), P(DP + MP, None), P(DP, None), P(DP, None), P(), P())
    out_specs = (P(DP, MP), P(DP, MP))
    return jax.shard_map(local, mesh=split, in_specs=in_specs, out_specs=out_specs, check_vma=False)
```

```python
import jax
import jax.numpy as jnp
from jax import lax
from jax.sharding import Mesh, PartitionSpec as P

SIZES = (8, 2, 2, 2, 4, 2)
NAMES = ("y", "a", "b", "zl", "x", "c")
DP = ("y", "a", "b")
MP = ("zl", "x", "c")
ROW = ("zl", "x")


def shifted(value, axis, steps):
    count = lax.axis_size(axis)
    return lax.ppermute(value, axis, [(s, (s + steps) % count) for s in range(count)])


def normalize(rows, axis=-1):
    wide = rows.astype(jnp.float32)
    factor = lax.rsqrt(jnp.sum(wide * wide, axis=axis, keepdims=True) + 1e-06)
    return (wide * factor, factor)


def unit_back(direction, unit, factor, axis=-1):
    return (direction - unit * jnp.sum(unit * direction, axis=axis, keepdims=True)) * factor


def gather(text, feat):
    rows = text.shape[0]
    far = shifted(jnp.concatenate([text, feat], axis=0), "a", 1)
    chunk = jnp.concatenate([text, far[:rows], feat, far[rows:]], axis=0)
    chunks = [chunk]
    up = down = chunk
    for _ in range(3):
        up, down = shifted(up, "y", 1), shifted(down, "y", -1)
        chunks += [up, down]
    half = chunk.shape[0] // 2
    last_text, last_feat = shifted(up[:half], "y", 1), shifted(down[half:], "y", -1)
    texts = jnp.concatenate([piece[:half] for piece in chunks] + [last_text], axis=0)
    feats = jnp.concatenate([piece[half:] for piece in chunks] + [last_feat], axis=0)
    return texts, shifted(texts, "c", 1), feats, shifted(feats, "c", 1)


def sum_over_row(slabs):
    got = lax.all_to_all(slabs, ROW, 0, 0, tiled=True)
    return jnp.sum(got.astype(jnp.float32), axis=0)


def sum_over_dp(parts):
    rows, cols = parts.shape
    got = lax.all_to_all(parts.astype(jnp.bfloat16).reshape(8, rows // 8, cols), "y", 0, 0, tiled=True)
    near = jnp.sum(got.astype(jnp.float32), axis=0)
    return jnp.sum(lax.all_to_all(near.reshape(4, rows // 32, cols), ("a", "b"), 0, 0, tiled=True), axis=0)


def local(image_emb, text_emb, image_feat, text_feat, logit_scale, logit_bias):
    column = lax.axis_index(MP)
    core = lax.axis_index("c")
    low = lax.axis_index("b")
    own_rows, width = text_emb.shape
    block = image_emb.shape[0]
    depth = image_feat.shape[1]
    cols = width // 16
    scale = logit_scale[0]
    offset = logit_bias[0]

    images = lax.ppermute(image_emb, ("b", "c"), [(0, 0), (1, 2), (2, 1), (3, 3)])
    own_feat = lax.dynamic_slice_in_dim(text_feat, column * own_rows, own_rows, 0)
    text_here, text_there, feat_here, feat_there = gather(text_emb, own_feat)

    image_unit, image_norm = normalize(images)
    image_low = image_unit.astype(jnp.bfloat16)
    texts = jnp.concatenate([text_here, text_there], axis=0)
    feats = jnp.concatenate([feat_here, feat_there], axis=0)
    text_unit, text_norm = normalize(texts)
    text_low = text_unit.astype(jnp.bfloat16)
    rows = text_low.shape[0]
    logits = lax.dot_general(text_low, image_low, (((1,), (1,)), ((), ())), preferred_element_type=jnp.float32)
    row_ids = jnp.arange(rows, dtype=jnp.int32)[:, None]
    image_ids = jnp.arange(block, dtype=jnp.int32)[None, :]
    other = column + 1 - 2 * core
    match = (row_ids < own_rows) & (image_ids == column * own_rows + row_ids)
    match |= (row_ids >= rows // 2) & (row_ids < rows // 2 + own_rows) & (
        image_ids == other * own_rows + row_ids - rows // 2
    )
    sign = jnp.where(match & (low == core), 1.0, -1.0).astype(jnp.float32)
    value = scale * logits + offset
    weights = (-scale * sign * jax.nn.sigmoid(-sign * value)).astype(jnp.bfloat16)

    image_dir = lax.dot_general(text_low, weights, (((0,), (0,)), ((), ())), preferred_element_type=jnp.float32)
    image_part = unit_back(image_dir, image_unit.T, image_norm.T, 0).astype(jnp.bfloat16)
    image_two = sum_over_row(image_part.reshape(8, 2 * cols, block)).reshape(2, cols, block)
    same = lax.dynamic_index_in_dim(image_two, low, 0, keepdims=False)
    cross = lax.dynamic_index_in_dim(image_two, 1 - low, 0, keepdims=False)
    same = lax.ppermute(same, ("b", "c"), [(0, 0), (1, 2), (2, 1), (3, 3)])
    cross = lax.ppermute(cross, ("b", "c"), [(0, 1), (1, 3), (2, 0), (3, 2)])
    image_cols = (same + cross).astype(jnp.bfloat16)
    image_term = jnp.dot(image_cols, image_feat, preferred_element_type=jnp.float32)

    text_dir = jnp.dot(weights, image_low, preferred_element_type=jnp.float32)
    text_part = unit_back(text_dir, text_unit, text_norm).astype(jnp.bfloat16)
    text_all = lax.dot_general(text_part, feats, (((0,), (0,)), ((), ())), preferred_element_type=jnp.float32)
    slabs = text_all.astype(jnp.bfloat16).reshape(8, 2, cols, depth)
    keep = lax.dynamic_index_in_dim(slabs, core, 1, keepdims=False).astype(jnp.float32)
    give = lax.dynamic_index_in_dim(slabs, 1 - core, 1, keepdims=False)
    text_term = sum_over_row((keep + shifted(give, "c", 1).astype(jnp.float32)).astype(jnp.bfloat16))

    own = sum_over_dp(jnp.concatenate([image_term, text_term], axis=0).T)
    return (own[:, :cols], own[:, cols:])


def solution(mesh):
    split = Mesh(mesh.devices.reshape(SIZES), NAMES)
    in_specs = (P(DP, None), P(DP + MP, None), P(DP, None), P(DP, None), P(), P())
    out_specs = (P(DP, MP), P(DP, MP))
    return jax.shard_map(local, mesh=split, in_specs=in_specs, out_specs=out_specs, check_vma=False)
```

```python
import jax
import jax.numpy as jnp
from jax import lax
from jax.sharding import Mesh, PartitionSpec as P

SIZES = (8, 2, 2, 2, 4, 2)
NAMES = ("y", "a", "b", "zl", "x", "c")
DP = ("y", "a", "b")
MP = ("zl", "x", "c")
ROW = ("zl", "x")


def shifted(value, axis, steps):
    count = lax.axis_size(axis)
    return lax.ppermute(value, axis, [(s, (s + steps) % count) for s in range(count)])


def normalize(rows, axis=-1):
    wide = rows.astype(jnp.float32)
    factor = lax.rsqrt(jnp.sum(wide * wide, axis=axis, keepdims=True) + 1e-06)
    return (wide * factor, factor)


def unit_back(direction, unit, factor, axis=-1):
    return (direction - unit * jnp.sum(unit * direction, axis=axis, keepdims=True)) * factor


def gather(text, feat):
    chunk = jnp.concatenate([text, shifted(text, "a", 1), feat, shifted(feat, "a", 1)], axis=0)
    chunks = [chunk]
    up = down = chunk
    for _ in range(3):
        up, down = shifted(up, "y", 1), shifted(down, "y", -1)
        chunks += [up, down]
    half = chunk.shape[0] // 2
    last_text, last_feat = shifted(up[:half], "y", 1), shifted(down[half:], "y", -1)
    texts = jnp.concatenate([piece[:half] for piece in chunks] + [last_text], axis=0)
    feats = jnp.concatenate([piece[half:] for piece in chunks] + [last_feat], axis=0)
    return chunk, texts, feats


def other_block(image_emb, after):
    core = lax.axis_index("c")
    half = image_emb.shape[0] // 2
    piece = lax.dynamic_slice_in_dim(image_emb, core * half, half, 0)
    piece, _ = lax.optimization_barrier((piece, after))
    mine = shifted(piece, "b", 1)
    theirs = shifted(mine, "c", 1)
    return [jnp.where(core == 0, mine, theirs), jnp.where(core == 0, theirs, mine)]


def sum_over_mp_row(full):
    core = lax.axis_index("c")
    slabs = full.reshape(8, 2, full.shape[0] // 16, full.shape[1])
    keep = lax.dynamic_index_in_dim(slabs, core, 1, keepdims=False).astype(jnp.float32)
    give = lax.dynamic_index_in_dim(slabs, 1 - core, 1, keepdims=False)
    both = (keep + shifted(give, "c", 1).astype(jnp.float32)).astype(jnp.bfloat16)
    got = lax.all_to_all(both, ROW, 0, 0, tiled=True)
    return jnp.sum(got.astype(jnp.float32), axis=0)


def sum_over_dp(parts):
    rows, cols = parts.shape
    own = rows // 32
    parts = parts.astype(jnp.bfloat16)
    main = parts[:, :128].reshape(32, own, 128)
    rest = parts[:, 128:].reshape(32, own * (cols - 128))
    rest = jnp.pad(rest, ((0, 0), (0, -rest.shape[1] % 128))).reshape(32, -1, 128)
    got = lax.all_to_all(jnp.concatenate([main, rest], axis=1), DP, 0, 0, tiled=True)
    total = jnp.sum(got.astype(jnp.float32), axis=0)
    tail = total[own:].reshape(-1)[: own * (cols - 128)].reshape(own, cols - 128)
    return jnp.concatenate([total[:own], tail], axis=1)


def local(image_emb, text_emb, image_feat, text_feat, logit_scale, logit_bias):
    column = lax.axis_index(MP)
    own_rows, width = text_emb.shape
    block = image_emb.shape[0]
    cols = width // 16
    scale = logit_scale[0]
    offset = logit_bias[0]

    own_feat = lax.dynamic_slice_in_dim(text_feat, column * own_rows, own_rows, 0)
    chunk, texts, feats = gather(text_emb, own_feat)
    images = jnp.concatenate([image_emb] + other_block(image_emb, chunk), axis=0)
    images_t = lax.optimization_barrier(images.T)

    image_unit, image_norm = normalize(images)
    image_low = image_unit.astype(jnp.bfloat16)
    image_unit_t, image_norm_t = normalize(images_t, 0)
    text_unit, text_norm = normalize(texts)
    text_low = text_unit.astype(jnp.bfloat16)
    rows = text_low.shape[0]
    logits = lax.dot_general(text_low, image_low, (((1,), (1,)), ((), ())), preferred_element_type=jnp.float32)
    row_ids = jnp.arange(rows, dtype=jnp.int32)[:, None]
    image_ids = jnp.arange(2 * block, dtype=jnp.int32)[None, :]
    match = (row_ids < own_rows) & (image_ids == column * own_rows + row_ids)
    sign = jnp.where(match, 1.0, -1.0).astype(jnp.float32)
    value = scale * logits + offset
    weights = (-scale * sign * jax.nn.sigmoid(-sign * value)).astype(jnp.bfloat16)

    image_dir = lax.dot_general(text_low, weights, (((0,), (0,)), ((), ())), preferred_element_type=jnp.float32)
    image_part = unit_back(image_dir, image_unit_t, image_norm_t, 0).astype(jnp.bfloat16)
    image_two = sum_over_mp_row(image_part)
    image_cols = image_two[:, :block] + shifted(image_two[:, block:], "b", 1)
    image_term = jnp.dot(image_cols.astype(jnp.bfloat16), image_feat, preferred_element_type=jnp.float32)

    text_dir = jnp.dot(weights, image_low, preferred_element_type=jnp.float32)
    text_part = unit_back(text_dir, text_unit, text_norm).astype(jnp.bfloat16)
    text_all = lax.dot_general(text_part, feats, (((0,), (0,)), ((), ())), preferred_element_type=jnp.float32)
    text_term = sum_over_mp_row(text_all.astype(jnp.bfloat16))

    own = sum_over_dp(jnp.concatenate([image_term, text_term], axis=0).T)
    return (own[:, :cols], own[:, cols:])


def solution(mesh):
    split = Mesh(mesh.devices.reshape(SIZES), NAMES)
    in_specs = (P(DP, None), P(DP + MP, None), P(DP, None), P(DP, None), P(), P())
    out_specs = (P(DP, MP), P(DP, MP))
    return jax.shard_map(local, mesh=split, in_specs=in_specs, out_specs=out_specs, check_vma=False)
```

```python
import jax
import jax.numpy as jnp
from jax import lax
from jax.sharding import Mesh, PartitionSpec as P

SIZES = (8, 2, 2, 2, 4, 2)
NAMES = ("y", "a", "b", "zl", "x", "c")
DP = ("y", "a", "b")
MP = ("zl", "x", "c")
ROW = ("zl", "x")


def shifted(value, axis, steps):
    count = lax.axis_size(axis)
    return lax.ppermute(value, axis, [(s, (s + steps) % count) for s in range(count)])


def after(value, other):
    return lax.optimization_barrier((value, other))[0]


def normalize(rows, axis=-1):
    wide = rows.astype(jnp.float32)
    factor = lax.rsqrt(jnp.sum(wide * wide, axis=axis, keepdims=True) + 1e-06)
    return (wide * factor, factor)


def unit_back(direction, unit, factor, axis=-1):
    return (direction - unit * jnp.sum(unit * direction, axis=axis, keepdims=True)) * factor


def ring_step(value, way):
    count = lax.axis_size("y")
    pairs = [(2 * s + c, 2 * ((s + way * (1 - 2 * c)) % count) + c) for s in range(count) for c in range(2)]
    return lax.ppermute(value, ("y", "c"), pairs)


def gather(text, feat, image_emb):
    rows = text.shape[0]
    own = jnp.concatenate([text, feat], axis=0)
    far = lax.ppermute(own, ("a", "b", "zl"), [(s, 7 - s) for s in range(8)])
    chunk = jnp.concatenate([text, far[:rows], feat, far[rows:]], axis=0)
    chunks = [chunk]
    core = lax.axis_index("c")
    part = image_emb.shape[0] // 2
    piece = lax.dynamic_slice_in_dim(image_emb, core * part, part, 0)
    mine = shifted(after(piece, chunk), "b", 1)
    up = down = chunk
    for _ in range(3):
        up, down = ring_step(up, 1), ring_step(down, -1)
        chunks += [up, down]
    theirs = shifted(mine, "c", 1)
    other = [jnp.where(core == 0, mine, theirs), jnp.where(core == 0, theirs, mine)]
    last = ring_step(up, 1)
    half = chunk.shape[0] // 2
    texts = jnp.concatenate([piece[:half] for piece in chunks], axis=0)
    feats = jnp.concatenate([piece[half:] for piece in chunks + [last]], axis=0)
    return texts, last[:half], feats, jnp.concatenate([image_emb] + other, axis=0)


def core_sum(full):
    core = lax.axis_index("c")
    slabs = full.reshape(8, 2, full.shape[0] // 16, full.shape[1])
    keep = lax.dynamic_index_in_dim(slabs, core, 1, keepdims=False).astype(jnp.float32)
    give = lax.dynamic_index_in_dim(slabs, 1 - core, 1, keepdims=False)
    return (keep + shifted(give, "c", 1).astype(jnp.float32)).astype(jnp.bfloat16)


def row_sum(slabs):
    got = lax.all_to_all(slabs, ROW, 0, 0, tiled=True)
    return jnp.sum(got.astype(jnp.float32), axis=0)


def sum_over_dp(parts):
    rows, cols = parts.shape
    own = rows // 32
    parts = parts.astype(jnp.bfloat16)
    main = parts[:, :128].reshape(32, own, 128)
    rest = parts[:, 128:].reshape(32, own * (cols - 128))
    rest = jnp.pad(rest, ((0, 0), (0, -rest.shape[1] % 128))).reshape(32, -1, 128)
    got = lax.all_to_all(jnp.concatenate([main, rest], axis=1), DP, 0, 0, tiled=True)
    total = jnp.sum(got.astype(jnp.float32), axis=0)
    tail = total[own:].reshape(-1)[: own * (cols - 128)].reshape(own, cols - 128)
    return jnp.concatenate([total[:own], tail], axis=1)


def local(image_emb, text_emb, image_feat, text_feat, logit_scale, logit_bias):
    column = lax.axis_index(MP)
    own_rows, width = text_emb.shape
    block = image_emb.shape[0]
    cols = width // 16
    scale = logit_scale[0]
    offset = logit_bias[0]

    own_feat = lax.dynamic_slice_in_dim(text_feat, column * own_rows, own_rows, 0)
    texts, last_text, feats, images = gather(text_emb, own_feat, image_emb)
    images_t = lax.optimization_barrier(images.T)

    image_unit, image_norm = normalize(images)
    image_low = image_unit.astype(jnp.bfloat16)
    image_unit_t, image_norm_t = normalize(images_t, 0)
    image_ids = jnp.arange(2 * block, dtype=jnp.int32)[None, :]

    def pair_weights(low, has_own):
        logits = lax.dot_general(low, image_low, (((1,), (1,)), ((), ())), preferred_element_type=jnp.float32)
        value = scale * logits + offset
        if not has_own:
            return (scale * jax.nn.sigmoid(value)).astype(jnp.bfloat16)
        row_ids = jnp.arange(low.shape[0], dtype=jnp.int32)[:, None]
        match = (row_ids < own_rows) & (image_ids == column * own_rows + row_ids)
        sign = jnp.where(match, 1.0, -1.0).astype(jnp.float32)
        return (-scale * sign * jax.nn.sigmoid(-sign * value)).astype(jnp.bfloat16)

    def image_direction(low, weights):
        return lax.dot_general(low, weights, (((0,), (0,)), ((), ())), preferred_element_type=jnp.float32)

    def text_gradient(unit, norm, weights):
        direction = jnp.dot(weights, image_low, preferred_element_type=jnp.float32)
        return unit_back(direction, unit, norm).astype(jnp.bfloat16)

    text_unit, text_norm = normalize(texts)
    text_low = text_unit.astype(jnp.bfloat16)
    weights = pair_weights(text_low, True)
    image_dir = image_direction(text_low, weights)

    last_text = after(last_text, image_dir)
    last_unit, last_norm = normalize(last_text)
    last_low = last_unit.astype(jnp.bfloat16)
    last_weights = pair_weights(last_low, False)
    image_dir = image_dir + image_direction(last_low, last_weights)
    image_part = unit_back(image_dir, image_unit_t, image_norm_t, 0).astype(jnp.bfloat16)
    image_slabs = core_sum(image_part)
    image_two = row_sum(image_slabs)
    image_cols = image_two[:, :block] + shifted(image_two[:, block:], "b", 1)
    image_term = jnp.dot(image_cols.astype(jnp.bfloat16), image_feat, preferred_element_type=jnp.float32)

    last_weights = after(last_weights, image_part)
    text_part = jnp.concatenate(
        [text_gradient(text_unit, text_norm, weights), text_gradient(last_unit, last_norm, last_weights)], axis=0
    )
    text_part = after(text_part, image_slabs)
    text_all = lax.dot_general(text_part, feats, (((0,), (0,)), ((), ())), preferred_element_type=jnp.float32)
    text_term = row_sum(core_sum(text_all.astype(jnp.bfloat16)))

    own = sum_over_dp(jnp.concatenate([image_term, text_term], axis=0).T)
    return (own[:, :cols], own[:, cols:])


def solution(mesh):
    split = Mesh(mesh.devices.reshape(SIZES), NAMES)
    in_specs = (P(DP, None), P(DP + MP, None), P(DP, None), P(DP, None), P(), P())
    out_specs = (P(DP, MP), P(DP, MP))
    return jax.shard_map(local, mesh=split, in_specs=in_specs, out_specs=out_specs, check_vma=False)
```

```python
import jax
import jax.numpy as jnp
from jax import lax
from jax.sharding import Mesh, PartitionSpec as P

SIZES = (8, 2, 2, 2, 4, 2)
NAMES = ("y", "a", "b", "zl", "x", "c")
DP = ("y", "a", "b")
MP = ("zl", "x", "c")
ROW = ("zl", "x")


def shifted(value, axis, steps):
    count = lax.axis_size(axis)
    return lax.ppermute(value, axis, [(s, (s + steps) % count) for s in range(count)])


def after(value, other):
    return lax.optimization_barrier((value, other))[0]


def normalize(rows, axis=-1):
    wide = rows.astype(jnp.float32)
    factor = lax.rsqrt(jnp.sum(wide * wide, axis=axis, keepdims=True) + 1e-06)
    return (wide * factor, factor)


def unit_back(direction, unit, factor, axis=-1):
    return (direction - unit * jnp.sum(unit * direction, axis=axis, keepdims=True)) * factor


def ring_step(value, way):
    count = lax.axis_size("y")
    pairs = [(2 * s + c, 2 * ((s + way * (1 - 2 * c)) % count) + c) for s in range(count) for c in range(2)]
    return lax.ppermute(value, ("y", "c"), pairs)


def gather(text, feat, image_emb):
    rows = text.shape[0]
    own = lax.optimization_barrier(jnp.concatenate([text, feat], axis=0))
    text, feat = own[:rows], own[rows:]
    far = lax.ppermute(own, ("a", "b", "zl"), [(s, 7 - s) for s in range(8)])
    chunk = jnp.concatenate([text, far[:rows], feat, far[rows:]], axis=0)
    chunks = [chunk]
    core = lax.axis_index("c")
    part = image_emb.shape[0] // 2
    piece = lax.dynamic_slice_in_dim(image_emb, core * part, part, 0)
    mine = shifted(after(piece, chunk), "b", 1)
    up = down = chunk
    for _ in range(3):
        up, down = ring_step(up, 1), ring_step(down, -1)
        chunks += [up, down]
    mine = after(mine, up)
    theirs = shifted(mine, "c", 1)
    other = [jnp.where(core == 0, mine, theirs), jnp.where(core == 0, theirs, mine)]
    last = ring_step(down, -1)
    half = chunk.shape[0] // 2
    texts = jnp.concatenate([piece[:half] for piece in chunks], axis=0)
    feats = jnp.concatenate([piece[half:] for piece in chunks], axis=0)
    return texts, feats, last, jnp.concatenate([image_emb] + other, axis=0)


def core_sum(full):
    core = lax.axis_index("c")
    slabs = full.reshape(8, 2, full.shape[0] // 16, full.shape[1])
    keep = lax.dynamic_index_in_dim(slabs, core, 1, keepdims=False).astype(jnp.float32)
    give = lax.dynamic_index_in_dim(slabs, 1 - core, 1, keepdims=False)
    return (keep + shifted(give, "c", 1).astype(jnp.float32)).astype(jnp.bfloat16)


def row_sum(slabs):
    got = lax.all_to_all(slabs, ROW, 0, 0, tiled=True)
    return jnp.sum(got.astype(jnp.float32), axis=0)


def sum_over_dp(parts):
    rows, cols = parts.shape
    own = rows // 32
    parts = parts.astype(jnp.bfloat16)
    main = parts[:, :128].reshape(32, own, 128)
    rest = parts[:, 128:].reshape(32, own * (cols - 128))
    rest = jnp.pad(rest, ((0, 0), (0, -rest.shape[1] % 128))).reshape(32, -1, 128)
    got = lax.all_to_all(jnp.concatenate([main, rest], axis=1), DP, 0, 0, tiled=True)
    total = jnp.sum(got.astype(jnp.float32), axis=0)
    tail = total[own:].reshape(-1)[: own * (cols - 128)].reshape(own, cols - 128)
    return jnp.concatenate([total[:own], tail], axis=1)


def local(image_emb, text_emb, image_feat, text_feat, logit_scale, logit_bias):
    column = lax.axis_index(MP)
    own_rows, width = text_emb.shape
    block = image_emb.shape[0]
    cols = width // 16
    scale = logit_scale[0]
    offset = logit_bias[0]

    own_feat = lax.dynamic_slice_in_dim(text_feat, column * own_rows, own_rows, 0)
    texts, feats, last, images = gather(text_emb, own_feat, image_emb)
    images_t = lax.optimization_barrier(images.T)

    image_unit, image_norm = normalize(images)
    image_low = image_unit.astype(jnp.bfloat16)
    image_unit_t, image_norm_t = normalize(images_t, 0)
    image_ids = jnp.arange(2 * block, dtype=jnp.int32)[None, :]

    def pair_weights(low, has_own):
        logits = lax.dot_general(low, image_low, (((1,), (1,)), ((), ())), preferred_element_type=jnp.float32)
        value = scale * logits + offset
        if not has_own:
            return (scale * jax.nn.sigmoid(value)).astype(jnp.bfloat16)
        row_ids = jnp.arange(low.shape[0], dtype=jnp.int32)[:, None]
        match = (row_ids < own_rows) & (image_ids == column * own_rows + row_ids)
        sign = jnp.where(match, 1.0, -1.0).astype(jnp.float32)
        return (-scale * sign * jax.nn.sigmoid(-sign * value)).astype(jnp.bfloat16)

    def image_direction(low, weights):
        return lax.dot_general(low, weights, (((0,), (0,)), ((), ())), preferred_element_type=jnp.float32)

    def text_gradient(unit, norm, weights):
        direction = jnp.dot(weights, image_low, preferred_element_type=jnp.float32)
        return unit_back(direction, unit, norm).astype(jnp.bfloat16)

    text_unit, text_norm = normalize(texts)
    text_low = text_unit.astype(jnp.bfloat16)
    weights = pair_weights(text_low, True)
    image_dir = image_direction(text_low, weights)

    last = after(last, image_dir)
    half = last.shape[0] // 2
    last_unit, last_norm = normalize(last[:half])
    last_low = last_unit.astype(jnp.bfloat16)
    last_weights = pair_weights(last_low, False)
    image_dir = image_dir + image_direction(last_low, last_weights)
    image_part = unit_back(image_dir, image_unit_t, image_norm_t, 0).astype(jnp.bfloat16)
    image_slabs = core_sum(image_part)
    image_two = row_sum(image_slabs)
    image_cols = image_two[:, :block] + shifted(image_two[:, block:], "b", 1)
    image_term = jnp.dot(image_cols.astype(jnp.bfloat16), image_feat, preferred_element_type=jnp.float32)

    weights, last_weights = after((weights, last_weights), image_part)
    parts = (text_gradient(text_unit, text_norm, weights), text_gradient(last_unit, last_norm, last_weights))
    parts, last_feat = after((parts, last[half:]), image_slabs)
    feats = jnp.concatenate([feats, last_feat], axis=0)
    text_all = lax.dot_general(
        jnp.concatenate(parts, axis=0), feats, (((0,), (0,)), ((), ())), preferred_element_type=jnp.float32
    )
    text_term = row_sum(core_sum(text_all.astype(jnp.bfloat16)))

    own = sum_over_dp(jnp.concatenate([image_term, text_term], axis=0).T)
    return (own[:, :cols], own[:, cols:])


def solution(mesh):
    split = Mesh(mesh.devices.reshape(SIZES), NAMES)
    in_specs = (P(DP, None), P(DP + MP, None), P(DP, None), P(DP, None), P(), P())
    out_specs = (P(DP, MP), P(DP, MP))
    return jax.shard_map(local, mesh=split, in_specs=in_specs, out_specs=out_specs, check_vma=False)
```

```python
import jax
import jax.numpy as jnp
from jax import lax
from jax.sharding import Mesh, PartitionSpec as P

SIZES = (8, 2, 2, 2, 4, 2)
NAMES = ("y", "a", "b", "zl", "x", "c")
DP = ("y", "a", "b")
MP = ("zl", "x", "c")
ROW = ("zl", "x")


def shifted(value, axis, steps):
    count = lax.axis_size(axis)
    return lax.ppermute(value, axis, [(s, (s + steps) % count) for s in range(count)])


def after(value, other):
    return lax.optimization_barrier((value, other))[0]


def normalize(rows, axis=-1):
    wide = rows.astype(jnp.float32)
    factor = lax.rsqrt(jnp.sum(wide * wide, axis=axis, keepdims=True) + 1e-06)
    return (wide * factor, factor)


def unit_back(direction, unit, factor, axis=-1):
    return (direction - unit * jnp.sum(unit * direction, axis=axis, keepdims=True)) * factor


def ring_step(value, way):
    count = lax.axis_size("y")
    pairs = [(2 * s + c, 2 * ((s + way * (1 - 2 * c)) % count) + c) for s in range(count) for c in range(2)]
    return lax.ppermute(value, ("y", "c"), pairs)


def gather(text, feat, image_emb):
    rows = text.shape[0]
    own = lax.optimization_barrier(jnp.concatenate([text, feat], axis=0))
    text, feat = own[:rows], own[rows:]
    core = lax.axis_index("c")
    part = image_emb.shape[0] // 2
    piece = lax.dynamic_slice_in_dim(image_emb, core * part, part, 0)
    far = lax.ppermute(own, ("a", "b", "zl"), [(s, 7 - s) for s in range(8)])
    far, piece, own = lax.optimization_barrier((far, piece, own))
    text, feat = own[:rows], own[rows:]
    chunk = jnp.concatenate([text, far[:rows], feat, far[rows:]], axis=0)
    chunks = [chunk]
    mine = shifted(piece, "b", 1)
    up = down = chunk
    for _ in range(3):
        up, down = ring_step(up, 1), ring_step(down, -1)
        chunks += [up, down]
    mine = after(mine, up)
    theirs = shifted(mine, "c", 1)
    other = [jnp.where(core == 0, mine, theirs), jnp.where(core == 0, theirs, mine)]
    last = ring_step(down, -1)
    half = chunk.shape[0] // 2
    texts = jnp.concatenate([piece[:half] for piece in chunks], axis=0)
    feats = jnp.concatenate([piece[half:] for piece in chunks], axis=0)
    return texts, feats, last, jnp.concatenate([image_emb] + other, axis=0)


def core_sum(full):
    core = lax.axis_index("c")
    slabs = full.reshape(8, 2, full.shape[0] // 16, full.shape[1])
    keep = lax.dynamic_index_in_dim(slabs, core, 1, keepdims=False).astype(jnp.float32)
    give = lax.dynamic_index_in_dim(slabs, 1 - core, 1, keepdims=False)
    return (keep + shifted(give, "c", 1).astype(jnp.float32)).astype(jnp.bfloat16)


def row_sum(slabs):
    got = lax.all_to_all(slabs, ROW, 0, 0, tiled=True)
    return jnp.sum(got.astype(jnp.float32), axis=0)


def sum_over_dp(parts):
    rows, cols = parts.shape
    own = rows // 32
    parts = parts.astype(jnp.bfloat16)
    main = parts[:, :128].reshape(32, own, 128)
    rest = parts[:, 128:].reshape(32, own * (cols - 128))
    rest = jnp.pad(rest, ((0, 0), (0, -rest.shape[1] % 128))).reshape(32, -1, 128)
    got = lax.all_to_all(jnp.concatenate([main, rest], axis=1), DP, 0, 0, tiled=True)
    total = jnp.sum(got.astype(jnp.float32), axis=0)
    tail = total[own:].reshape(-1)[: own * (cols - 128)].reshape(own, cols - 128)
    return jnp.concatenate([total[:own], tail], axis=1)


def local(image_emb, text_emb, image_feat, text_feat, logit_scale, logit_bias):
    column = lax.axis_index(MP)
    own_rows, width = text_emb.shape
    block = image_emb.shape[0]
    cols = width // 16
    scale = logit_scale[0]
    offset = logit_bias[0]

    own_feat = lax.dynamic_slice_in_dim(text_feat, column * own_rows, own_rows, 0)
    texts, feats, last, images = gather(text_emb, own_feat, image_emb)
    images_t = lax.optimization_barrier(images.T)

    image_unit, image_norm = normalize(images)
    image_low = image_unit.astype(jnp.bfloat16)
    image_unit_t, image_norm_t = normalize(images_t, 0)
    image_ids = jnp.arange(2 * block, dtype=jnp.int32)[None, :]

    def pair_weights(low, has_own):
        logits = lax.dot_general(low, image_low, (((1,), (1,)), ((), ())), preferred_element_type=jnp.float32)
        value = scale * logits + offset
        if not has_own:
            return (scale * jax.nn.sigmoid(value)).astype(jnp.bfloat16)
        row_ids = jnp.arange(low.shape[0], dtype=jnp.int32)[:, None]
        match = (row_ids < own_rows) & (image_ids == column * own_rows + row_ids)
        sign = jnp.where(match, 1.0, -1.0).astype(jnp.float32)
        return (-scale * sign * jax.nn.sigmoid(-sign * value)).astype(jnp.bfloat16)

    def image_direction(low, weights):
        return lax.dot_general(low, weights, (((0,), (0,)), ((), ())), preferred_element_type=jnp.float32)

    def text_gradient(unit, norm, weights):
        direction = jnp.dot(weights, image_low, preferred_element_type=jnp.float32)
        return unit_back(direction, unit, norm).astype(jnp.bfloat16)

    text_unit, text_norm = normalize(texts)
    text_low = text_unit.astype(jnp.bfloat16)
    weights = pair_weights(text_low, True)
    image_dir = image_direction(text_low, weights)

    last = after(last, image_dir)
    half = last.shape[0] // 2
    last_unit, last_norm = normalize(last[:half])
    last_low = last_unit.astype(jnp.bfloat16)
    last_weights = pair_weights(last_low, False)
    image_dir = image_dir + image_direction(last_low, last_weights)
    image_part = unit_back(image_dir, image_unit_t, image_norm_t, 0).astype(jnp.bfloat16)
    image_slabs = core_sum(image_part)
    image_two = row_sum(image_slabs)
    image_cols = image_two[:, :block] + shifted(image_two[:, block:], "b", 1)
    image_term = jnp.dot(image_cols.astype(jnp.bfloat16), image_feat, preferred_element_type=jnp.float32)

    weights, last_weights = after((weights, last_weights), image_part)
    parts = (text_gradient(text_unit, text_norm, weights), text_gradient(last_unit, last_norm, last_weights))
    parts, last_feat = after((parts, last[half:]), image_slabs)
    feats = jnp.concatenate([feats, last_feat], axis=0)
    text_all = lax.dot_general(
        jnp.concatenate(parts, axis=0), feats, (((0,), (0,)), ((), ())), preferred_element_type=jnp.float32
    )
    text_term = row_sum(core_sum(text_all.astype(jnp.bfloat16)))

    own = sum_over_dp(jnp.concatenate([image_term, text_term], axis=0).T)
    return (own[:, :cols], own[:, cols:])


def solution(mesh):
    split = Mesh(mesh.devices.reshape(SIZES), NAMES)
    in_specs = (P(DP, None), P(DP + MP, None), P(DP, None), P(DP, None), P(), P())
    out_specs = (P(DP, MP), P(DP, MP))
    return jax.shard_map(local, mesh=split, in_specs=in_specs, out_specs=out_specs, check_vma=False)
```

```python
import jax
import jax.numpy as jnp
from jax import lax
from jax.sharding import Mesh, PartitionSpec as P

SIZES = (8, 2, 2, 2, 4, 2)
NAMES = ("y", "a", "b", "zl", "x", "c")
DP = ("y", "a", "b")
MP = ("zl", "x", "c")
ROW = ("zl", "x")


def shifted(value, axis, steps):
    count = lax.axis_size(axis)
    return lax.ppermute(value, axis, [(s, (s + steps) % count) for s in range(count)])


def after(value, other):
    return lax.optimization_barrier((value, other))[0]


def normalize(rows, axis=-1):
    wide = rows.astype(jnp.float32)
    factor = lax.rsqrt(jnp.sum(wide * wide, axis=axis, keepdims=True) + 1e-06)
    return (wide * factor, factor)


def unit_back(direction, unit, factor, axis=-1):
    return (direction - unit * jnp.sum(unit * direction, axis=axis, keepdims=True)) * factor


def ring_step(value, way):
    count = lax.axis_size("y")
    pairs = [(2 * s + c, 2 * ((s + way * (1 - 2 * c)) % count) + c) for s in range(count) for c in range(2)]
    return lax.ppermute(value, ("y", "c"), pairs)


def gather(text, feat, image_emb):
    rows = text.shape[0]
    own = lax.optimization_barrier(jnp.concatenate([text, feat], axis=0))
    text, feat = own[:rows], own[rows:]
    core = lax.axis_index("c")
    part = image_emb.shape[0] // 2
    piece = lax.dynamic_slice_in_dim(image_emb, core * part, part, 0)
    far = lax.ppermute(own, ("a", "b", "zl"), [(s, 7 - s) for s in range(8)])
    far, piece, own = lax.optimization_barrier((far, piece, own))
    text, feat = own[:rows], own[rows:]
    chunk = jnp.concatenate([text, far[:rows], feat, far[rows:]], axis=0)
    chunks = [chunk]
    mine = shifted(piece, "b", 1)
    up = down = chunk
    for _ in range(3):
        up, down = ring_step(up, 1), ring_step(down, -1)
        chunks += [up, down]
    mine = after(mine, up)
    theirs = shifted(mine, "c", 1)
    other = [jnp.where(core == 0, mine, theirs), jnp.where(core == 0, theirs, mine)]
    last = ring_step(down, -1)
    half = chunk.shape[0] // 2
    texts = jnp.concatenate([piece[:half] for piece in chunks], axis=0)
    feats = jnp.concatenate([piece[half:] for piece in chunks], axis=0)
    return texts, feats, last, jnp.concatenate([image_emb] + other, axis=0)


def core_sum(full):
    core = lax.axis_index("c")
    slabs = full.reshape(8, 2, full.shape[0] // 16, full.shape[1])
    keep = lax.dynamic_index_in_dim(slabs, core, 1, keepdims=False).astype(jnp.float32)
    give = lax.dynamic_index_in_dim(slabs, 1 - core, 1, keepdims=False)
    return (keep + shifted(give, "c", 1).astype(jnp.float32)).astype(jnp.bfloat16)


def row_sum(slabs):
    got = lax.all_to_all(slabs, ROW, 0, 0, tiled=True)
    return jnp.sum(got.astype(jnp.float32), axis=0)


def sum_over_dp(parts):
    rows, cols = parts.shape
    own = rows // 32
    parts = parts.astype(jnp.bfloat16)
    main = parts[:, :128].reshape(32, own, 128)
    rest = parts[:, 128:].reshape(32, own * (cols - 128))
    rest = jnp.pad(rest, ((0, 0), (0, -rest.shape[1] % 128))).reshape(32, -1, 128)
    got = lax.all_to_all(jnp.concatenate([main, rest], axis=1), DP, 0, 0, tiled=True)
    total = jnp.sum(got.astype(jnp.float32), axis=0)
    tail = total[own:].reshape(-1)[: own * (cols - 128)].reshape(own, cols - 128)
    return jnp.concatenate([total[:own], tail], axis=1)


def local(image_emb, text_emb, image_feat, text_feat, logit_scale, logit_bias):
    column = lax.axis_index(MP)
    own_rows, width = text_emb.shape
    block = image_emb.shape[0]
    cols = width // 16
    scale = logit_scale[0]
    offset = logit_bias[0]

    own_feat = lax.dynamic_slice_in_dim(text_feat, column * own_rows, own_rows, 0)
    texts, feats, last, images = gather(text_emb, own_feat, image_emb)
    images_t = lax.optimization_barrier(images.T)

    image_unit, image_norm = normalize(images)
    image_low = image_unit.astype(jnp.bfloat16)
    image_unit_t, image_norm_t = normalize(images_t, 0)
    image_ids = jnp.arange(2 * block, dtype=jnp.int32)[None, :]

    def pair_weights(low, has_own):
        logits = lax.dot_general(low, image_low, (((1,), (1,)), ((), ())), preferred_element_type=jnp.float32)
        value = scale * logits + offset
        if not has_own:
            return (scale * jax.nn.sigmoid(value)).astype(jnp.bfloat16)
        row_ids = jnp.arange(low.shape[0], dtype=jnp.int32)[:, None]
        match = (row_ids < own_rows) & (image_ids == column * own_rows + row_ids)
        sign = jnp.where(match, 1.0, -1.0).astype(jnp.float32)
        return (-scale * sign * jax.nn.sigmoid(-sign * value)).astype(jnp.bfloat16)

    def image_direction(low, weights):
        return lax.dot_general(low, weights, (((0,), (0,)), ((), ())), preferred_element_type=jnp.float32)

    def text_gradient(unit, norm, weights):
        direction = jnp.dot(weights, image_low, preferred_element_type=jnp.float32)
        return unit_back(direction, unit, norm).astype(jnp.bfloat16)

    text_unit, text_norm = normalize(texts)
    text_low = text_unit.astype(jnp.bfloat16)
    weights = pair_weights(text_low, True)
    image_dir = image_direction(text_low, weights)

    last = after(last, image_dir)
    half = last.shape[0] // 2
    last_unit, last_norm = normalize(last[:half])
    last_low = last_unit.astype(jnp.bfloat16)
    last_weights = pair_weights(last_low, False)
    image_dir = image_dir + image_direction(last_low, last_weights)
    image_part = unit_back(image_dir, image_unit_t, image_norm_t, 0).astype(jnp.bfloat16)
    image_slabs = core_sum(image_part)
    image_two = row_sum(image_slabs)
    far_sums = shifted(image_two[:, block:].astype(jnp.bfloat16), "b", 1)
    image_cols = image_two[:, :block] + far_sums.astype(jnp.float32)
    image_term = jnp.dot(image_cols.astype(jnp.bfloat16), image_feat, preferred_element_type=jnp.float32)

    weights, last_weights = after((weights, last_weights), image_part)
    parts = (text_gradient(text_unit, text_norm, weights), text_gradient(last_unit, last_norm, last_weights))
    parts, last_feat = after((parts, last[half:]), image_slabs)
    feats = jnp.concatenate([feats, last_feat], axis=0)
    text_all = lax.dot_general(
        jnp.concatenate(parts, axis=0), feats, (((0,), (0,)), ((), ())), preferred_element_type=jnp.float32
    )
    text_term = row_sum(core_sum(text_all.astype(jnp.bfloat16)))

    own = sum_over_dp(jnp.concatenate([image_term, text_term], axis=0).T)
    return (own[:, :cols], own[:, cols:])


def solution(mesh):
    split = Mesh(mesh.devices.reshape(SIZES), NAMES)
    in_specs = (P(DP, None), P(DP + MP, None), P(DP, None), P(DP, None), P(), P())
    out_specs = (P(DP, MP), P(DP, MP))
    return jax.shard_map(local, mesh=split, in_specs=in_specs, out_specs=out_specs, check_vma=False)
```
